32 devices in a mesh: leaf: 8 (over y, x, core), mat: 4 (over z).
Axes of the slice: x: 2, y: 2, z: 4, core: 2. Of those that a mesh axis runs over, the one named last changes fastest.
Arguments:
- leaf_value: float32 [64, 1024, 1024], P('leaf', 'mat'), as said below
- section_cost: float32 [1024, 1024], P('mat'), as said below
- input_cost: float32 [256, 256], replicated, as said below
- dynamics: float32 [1024, 1024], P('mat'), may hold values from -0.1875 to 0.1875
- input_map: float32 [1024, 256], replicated, may hold values from -0.1875 to 0.1875
- parent_of: int32 [64], replicated, may hold values from 0 to 15, as said below
- prob_weight: int32 [64], replicated, may hold values from 1 to 16
- parent_state: float32 [16, 1024], P('leaf', 'mat'), may hold values from -6 to 6
- disturbance: float32 [64, 1024], P('leaf', 'mat'), may hold values from -6 to 6
Outputs:
- parent_value: float32 [16, 1024, 1024], P('leaf', 'mat')
- parent_gain: float32 [16, 1024, 256], P('leaf', 'mat')
- child_state: float32 [64, 1024], P('leaf', 'mat')
The draws below stay inside these ranges and needn't reach their ends.
Inputs may be any that keep to these rules, and one draw needn't show every extreme that they name: Each leaf_value[l] is symmetric positive definite. `section_cost`: symmetric positive definite. `input_cost`: symmetric positive definite. `parent_of`: every parent has exactly 4 children; the parent of a leaf among the 8 leaves of one leaf index is one of that index's 2 parents, the last parent of the index before, or the first parent of the index after; each leaf index except the ends holds a child of both neighbours' parents.
All inputs are finite; a program needn't handle non-finite values.
Results may differ from the reference program's by a relative error of at most 0.000075.
Values sent between devices are 32-bit elements; how exact they have to be, the bound alone decides.
A program may use at most 64 MiB of HBM per device.

```python
import jax
import jax.numpy as jnp
from jax import lax

N = 1024
M = 256
LEAF_DEV = 8
LEAVES = 64
PARENTS = 16


def spd_matrix(key, order, spread, low, high):
    first, second = jax.random.split(key)
    noise = jax.random.normal(first, (order, order), jnp.float32) * (spread / order ** 0.5)
    sym = (noise + noise.T) * 0.7071
    diag = jax.random.uniform(second, (order,), jnp.float32, low, high)
    return sym + jnp.diag(diag)


def draw_leaf_value(key, part):
    base = jax.random.fold_in(key, 101)
    keys = jax.random.split(base, LEAVES)
    return jax.vmap(lambda k: spd_matrix(k, N, 0.7, 2.0, 4.0))(keys)


def draw_section_cost(key, part):
    base = jax.random.fold_in(key, 202)
    return spd_matrix(base, N, 0.3, 1.0, 2.0)


def draw_input_cost(key, part):
    base = jax.random.fold_in(key, 303)
    return spd_matrix(base, M, 0.3, 1.0, 3.0)


def draw_parent_of(key, part):
    base = jax.random.fold_in(key, 404)
    first, second = jax.random.split(base)
    groups = LEAVES // LEAF_DEV
    labels = jnp.arange(LEAVES, dtype=jnp.int32) // 4
    bounds = jnp.arange(groups - 1, dtype=jnp.int32)
    upper = jax.random.randint(first, (groups - 1,), 2, 4, dtype=jnp.int32) + (LEAF_DEV - 4)
    lower = jax.random.randint(second, (groups - 1,), 0, 2, dtype=jnp.int32)
    source = bounds * LEAF_DEV + upper
    target = (bounds + 1) * LEAF_DEV + lower
    return labels.at[source].set(labels[target]).at[target].set(labels[source])


def with_ends(result, rng, low, largest):
    shape = result.shape
    index_at = [jax.random.randint(jax.random.fold_in(rng, axis), (), 0, shape[axis]) for axis in range(len(shape))]
    result = result.at[tuple(index_at)].set(low)
    longest = shape.index(max(shape))
    index_at[longest] = (index_at[longest] + 1) % shape[longest]
    return result.at[tuple(index_at)].set(largest)


def steps_of(rng, dims, cuts, low, largest):
    loudness = 1.0
    for position, shards_of in cuts:
        draws = jax.random.uniform(jax.random.fold_in(jax.random.fold_in(rng, 6), position), (shards_of,), jnp.float32, low / len(cuts), largest / len(cuts))
        loudness = loudness * jnp.repeat(jnp.exp(draws), dims[position] // shards_of).reshape((-1,) + (1,) * (len(dims) - 1 - position))
    return loudness


def gaussian(key, extent, width, most, shards=(), kind=jnp.bfloat16):
    values = jax.random.normal(key, extent, jnp.float32) * width
    if len(shards) > 0:
        values = steps_of(key, extent, shards, -0.22, 0.18) * values
    return jnp.clip(values, min=-most, max=most).astype(kind)


def setup_inputs(seed: int = 0) -> dict:
    key_list = jax.random.split(jax.random.key(seed), 10)
    leaf_value = draw_leaf_value(jax.random.fold_in(key_list[9], 71), 0)
    section_cost = draw_section_cost(jax.random.fold_in(key_list[9], 71), 0)
    input_cost = draw_input_cost(jax.random.fold_in(key_list[9], 71), 0)
    dynamics = gaussian(key_list[3], (N, N), N ** -0.5, 0.1875, ((0, 4),), jnp.float32)
    input_map = gaussian(key_list[4], (N, M), N ** -0.5, 0.1875, (), jnp.float32)
    parent_of = draw_parent_of(jax.random.fold_in(key_list[9], 71), 0)
    prob_weight = with_ends(jax.random.randint(key_list[6], (LEAVES,), 1, 17), jax.random.fold_in(key_list[6], 1), 1, 16).astype(jnp.int32)
    parent_state = gaussian(key_list[7], (PARENTS, N), 1.0, 6.0, ((0, 8), (1, 4)), jnp.float32)
    disturbance = gaussian(key_list[8], (LEAVES, N), 1.0, 6.0, ((0, 8), (1, 4)), jnp.float32)
    return dict(leaf_value=leaf_value, section_cost=section_cost, input_cost=input_cost, dynamics=dynamics, input_map=input_map, parent_of=parent_of, prob_weight=prob_weight, parent_state=parent_state, disturbance=disturbance)


highest = lax.Precision.HIGHEST

def reference(leaf_value, section_cost, input_cost, dynamics, input_map, parent_of, prob_weight, parent_state, disturbance):
    weights = prob_weight.astype(jnp.float32)
    labels = jnp.arange(PARENTS, dtype=jnp.int32)
    member = jnp.where(parent_of[None, :] == labels[:, None], weights[None, :], jnp.zeros((), jnp.float32))
    totals = jnp.sum(member, axis=1)

    def per_parent(inputs):
        member_row, parent_total, own_state = inputs
        summed = jnp.einsum('l,lij->ij', member_row, leaf_value, precision=highest)
        expected = summed / parent_total
        propagated = jnp.dot(expected, dynamics, precision=highest)
        curvature = jnp.dot(dynamics.T, propagated, precision=highest)
        coupling = jnp.dot(input_map.T, propagated, precision=highest)
        hessian = input_cost + jnp.dot(input_map.T, jnp.dot(expected, input_map, precision=highest), precision=highest)
        factor = jnp.linalg.cholesky(hessian)
        scaled = lax.linalg.triangular_solve(factor, coupling, left_side=True, lower=True)
        feedback = -lax.linalg.triangular_solve(factor, scaled, left_side=True, lower=True, transpose_a=True)
        new_value = section_cost + curvature - jnp.dot(scaled.T, scaled, precision=highest)
        control = jnp.dot(feedback, own_state, precision=highest)
        following = jnp.dot(dynamics, own_state, precision=highest) + jnp.dot(input_map, control, precision=highest)
        return (new_value, feedback, following)
    new_values, gains, following = lax.map(per_parent, (member, totals, parent_state))
    child_state = following[parent_of] + disturbance
    return (new_values, jnp.swapaxes(gains, 1, 2), child_state)
```

```python
import jax
import jax.numpy as jnp
from jax import lax
from jax.experimental import pallas as pl
from jax.experimental.pallas import tpu as pltpu
from jax.sharding import PartitionSpec as P

highest = lax.Precision.HIGHEST
high = lax.Precision.HIGH


def shifted(block, axis, step):
    count = lax.axis_size(axis)
    return lax.ppermute(block, axis, [(i, (i + step) % count) for i in range(count)])


def shifts_of(count):
    order = []
    for step in range(1, count // 2 + 1):
        order.append(step)
        if count - step != step:
            order.append(count - step)
    return order


def gathered(block, axis, dim):
    count, me, size = lax.axis_size(axis), lax.axis_index(axis), block.shape[dim]
    shape = block.shape[:dim] + (size * count,) + block.shape[dim + 1 :]
    whole = lax.dynamic_update_slice_in_dim(jnp.zeros(shape, block.dtype), block, me * size, dim)
    parts = [(step, shifted(block, axis, step)) for step in shifts_of(count)]
    for step, part in parts:
        source = lax.rem(me + count - step, count)
        whole = lax.dynamic_update_slice_in_dim(whole, part, source * size, dim)
    return whole


def edge_rows(block):
    count = lax.axis_size("leaf")
    forward = [(i, i + 1) for i in range(count - 1)]
    backward = [(target, source) for source, target in forward]
    return forward, backward


def leaf_sum_kernel(member_ref, leaf_ref, low_ref, own_ref, high_ref):
    leaves = leaf_ref.shape[0]
    slots = own_ref.shape[0] + 2
    outs = [low_ref.at[0]] + [own_ref.at[t] for t in range(slots - 2)] + [high_ref.at[0]]
    for row in range(0, leaf_ref.shape[1], 8):
        terms = [leaf_ref[s, row : row + 8, :] for s in range(leaves)]
        for t in range(slots):
            total = terms[0] * member_ref[0, t]
            for s in range(1, leaves):
                total = total + terms[s] * member_ref[s, t]
            outs[t][row : row + 8, :] = total


def leaf_sums(member, leaf_value, par_dev):
    leaves, rows, states = leaf_value.shape
    tile = min(32, rows)
    block = lambda count: pl.BlockSpec((count, tile, states), lambda i: (0, i, 0))
    shape = lambda count: jax.ShapeDtypeStruct((count, rows, states), jnp.float32)
    return pl.pallas_call(
        leaf_sum_kernel,
        grid=(rows // tile,),
        in_specs=[pl.BlockSpec(memory_space=pltpu.SMEM), block(leaves)],
        out_specs=[block(1), block(par_dev), block(1)],
        out_shape=[shape(1), shape(par_dev), shape(1)],
        compiler_params=pltpu.CompilerParams(vmem_limit_bytes=32 * 2**20),
    )(member, leaf_value)


def inverse_kernel(cost_ref, map_ref, side_ref, inv_ref, hess):
    parents, _, inputs = side_ref.shape
    row = lax.broadcasted_iota(jnp.int32, (inputs, inputs), 0)
    col = lax.broadcasted_iota(jnp.int32, (inputs, inputs), 1)
    eye = (row == col).astype(jnp.float32)
    dot = lambda a, b: jnp.dot(a, b, precision=highest, preferred_element_type=jnp.float32)
    for p in range(parents):
        product = lax.dot_general(
            map_ref[...],
            side_ref[p],
            (((0,), (0,)), ((), ())),
            precision=highest,
            preferred_element_type=jnp.float32,
        )
        value = cost_ref[...] + product
        hess[p] = value
        bound = jnp.max(jnp.sum(jnp.abs(value), axis=0))
        inv_ref[p] = eye / bound

    def more(carry):
        turn, worst = carry
        return jnp.logical_and(turn < 64, worst > 1e-8)

    def step(carry):
        turn, _ = carry
        residual = [eye - dot(hess[p], inv_ref[p]) for p in range(parents)]
        for p in range(parents):
            inv_ref[p] = inv_ref[p] + dot(inv_ref[p], residual[p])
        worst = jnp.sum(residual[0] * residual[0])
        for p in range(1, parents):
            worst = jnp.maximum(worst, jnp.sum(residual[p] * residual[p]))
        return turn + 1, worst

    lax.while_loop(more, step, (jnp.int32(0), jnp.float32(jnp.inf)))


def inverses(input_cost, input_map, side):
    parents, _, inputs = side.shape
    return pl.pallas_call(
        inverse_kernel,
        in_specs=[pl.BlockSpec(memory_space=pltpu.VMEM)] * 3,
        out_specs=pl.BlockSpec(memory_space=pltpu.VMEM),
        out_shape=jax.ShapeDtypeStruct((parents, inputs, inputs), jnp.float32),
        scratch_shapes=[pltpu.VMEM((parents, inputs, inputs), jnp.float32)],
        compiler_params=pltpu.CompilerParams(vmem_limit_bytes=32 * 2**20),
        cost_estimate=pl.CostEstimate(
            flops=600 * parents * inputs**3, bytes_accessed=4 * 2**20, transcendentals=0
        ),
    )(input_cost, input_map, side)


def local(
    leaf_value,
    section_cost,
    input_cost,
    dynamics,
    input_map,
    parent_of,
    prob_weight,
    parent_state,
    disturbance,
):
    leaf_dev = leaf_value.shape[0]
    par_dev = parent_state.shape[0]
    slab_rows = leaf_value.shape[1]
    leaf_index = lax.axis_index("leaf")
    column = lax.axis_index("mat")
    count = lax.axis_size("mat")
    forward, backward = edge_rows(parent_state)
    row_start = column * slab_rows
    full_dyn = gathered(dynamics, "mat", 0)
    weights = prob_weight.astype(jnp.float32)
    my_parents = lax.dynamic_slice_in_dim(parent_of, leaf_index * leaf_dev, leaf_dev, 0)
    my_weights = lax.dynamic_slice_in_dim(weights, leaf_index * leaf_dev, leaf_dev, 0)
    first_label = leaf_index * par_dev
    slot_ids = jnp.arange(par_dev + 2, dtype=jnp.int32)
    chosen = (my_parents - first_label + 1)[:, None] == slot_ids[None, :]
    member = jnp.where(chosen, my_weights[:, None], 0.0)
    labels = first_label + jnp.arange(par_dev, dtype=jnp.int32)
    totals = jnp.sum(
        jnp.where(parent_of[:, None] == labels[None, :], weights[:, None], 0.0), axis=0
    )
    low, own, top = leaf_sums(member, leaf_value, par_dev)
    from_low = lax.ppermute(top, "leaf", forward)
    from_high = lax.ppermute(low, "leaf", backward)
    pads = [jnp.zeros_like(own[:1])] * (par_dev - 1)
    beside = jnp.concatenate([from_low] + pads) + jnp.concatenate(pads + [from_high])
    expected = (own + beside) / totals[:, None, None]

    side_rows = jnp.einsum("prk,ka->pra", expected, input_map, precision=high)
    side = gathered(side_rows, "mat", 1)
    state = gathered(parent_state, "mat", 1)

    def value_block(target):
        columns = lax.dynamic_slice_in_dim(full_dyn, target * slab_rows, slab_rows, 1)
        return jnp.einsum("prk,kj->prj", expected, columns, precision=high)

    dyn_cols = lax.dynamic_slice_in_dim(full_dyn, row_start, slab_rows, 1)
    parts = []
    for step in shifts_of(count):
        block = value_block(lax.rem(column + step, count))
        parts.append((step, shifted(block, "mat", step)))
    shape = (par_dev, slab_rows * count, slab_rows)
    value_cols = lax.dynamic_update_slice_in_dim(
        jnp.zeros(shape, jnp.float32), value_block(column), row_start, 1
    )

    inv = inverses(input_cost, input_map, side)
    free_next = jnp.einsum("ij,pj->pi", full_dyn, state, precision=highest)
    pull = jnp.einsum("pka,pk->pa", side, free_next, precision=highest)
    control = -jnp.einsum("pab,pb->pa", inv, pull, precision=highest)
    input_rows = lax.dynamic_slice_in_dim(input_map, row_start, slab_rows, 0)
    following = lax.dynamic_slice_in_dim(free_next, row_start, slab_rows, 1) + jnp.einsum(
        "ra,pa->pr", input_rows, control, precision=highest
    )
    below = lax.ppermute(following[par_dev - 1 :], "leaf", forward)
    above = lax.ppermute(following[:1], "leaf", backward)

    coupling_rows = jnp.einsum("kr,pka->pra", dyn_cols, side, precision=high)
    gain_rows = -jnp.einsum("pra,pab->prb", coupling_rows, inv, precision=high)
    feedback = jnp.einsum("prb,pkb->prk", gain_rows, side, precision=high)

    for step, part in parts:
        source = lax.rem(column + count - step, count)
        value_cols = lax.dynamic_update_slice_in_dim(value_cols, part, source * slab_rows, 1)
    closed = jnp.swapaxes(value_cols, 1, 2) + feedback
    new_value = section_cost[None] + jnp.einsum("prk,kj->prj", closed, full_dyn, precision=high)

    extended = jnp.concatenate([below, following, above], axis=0)
    child_state = disturbance
    for t in range(par_dev + 2):
        child_state = child_state + jnp.where(chosen[:, t : t + 1], extended[t][None, :], 0.0)
    return (new_value, gain_rows, child_state)


def solution(mesh):
    in_specs = (
        P("leaf", "mat", None),
        P("mat", None),
        P(),
        P("mat", None),
        P(),
        P(),
        P(),
        P("leaf", "mat"),
        P("leaf", "mat"),
    )
    out_specs = (P("leaf", "mat", None), P("leaf", "mat", None), P("leaf", "mat"))
    return jax.shard_map(local, mesh=mesh, in_specs=in_specs, out_specs=out_specs, check_vma=False)
```

```python
import jax
import jax.numpy as jnp
from jax import lax
from jax.experimental import pallas as pl
from jax.experimental.pallas import tpu as pltpu
from jax.sharding import PartitionSpec as P

highest = lax.Precision.HIGHEST
high = lax.Precision.HIGH


def shifted(block, axis, step):
    count = lax.axis_size(axis)
    return lax.ppermute(block, axis, [(i, (i + step) % count) for i in range(count)])


def shifts_of(count):
    order = []
    for step in range(1, count // 2 + 1):
        order.append(step)
        if count - step != step:
            order.append(count - step)
    return order


def gathered(block, axis, dim):
    count, me, size = lax.axis_size(axis), lax.axis_index(axis), block.shape[dim]
    shape = block.shape[:dim] + (size * count,) + block.shape[dim + 1 :]
    whole = lax.dynamic_update_slice_in_dim(jnp.zeros(shape, block.dtype), block, me * size, dim)
    parts = [(step, shifted(block, axis, step)) for step in shifts_of(count)]
    for step, part in parts:
        source = lax.rem(me + count - step, count)
        whole = lax.dynamic_update_slice_in_dim(whole, part, source * size, dim)
    return whole


def gathered_once(block):
    leaves, count = lax.axis_size("leaf"), lax.axis_size("mat")
    size = block.shape[0]
    if leaves % 4 or size % 32:
        return gathered(block, "mat", 0)
    half, quarter = leaves // 2, size // 4
    leaf, me = lax.axis_index("leaf"), lax.axis_index("mat")
    upper, core = leaf // half, lax.rem(leaf, 2)
    across = [(i, (i + half) % leaves) for i in range(leaves)]
    beside = [(i, i ^ 1) for i in range(leaves)]
    mine = lax.dynamic_slice_in_dim(block, (2 * upper + core) * quarter, quarter, 0)
    own = [(step, shifted(mine, "mat", step)) for step in shifts_of(count)]
    shape = (size * count,) + block.shape[1:]
    whole = lax.dynamic_update_slice_in_dim(jnp.zeros(shape, block.dtype), block, me * size, 0)
    for step, part in own:
        start = lax.rem(me + count - step, count) * size
        other = lax.ppermute(part, "leaf", across)
        pieces = (
            (part, upper, core),
            (other, 1 - upper, core),
            (lax.ppermute(part, "leaf", beside), upper, 1 - core),
            (lax.ppermute(other, "leaf", beside), 1 - upper, 1 - core),
        )
        for piece, high_half, side in pieces:
            at = start + (2 * high_half + side) * quarter
            whole = lax.dynamic_update_slice_in_dim(whole, piece, at, 0)
    return whole


def edge_rows(block):
    count = lax.axis_size("leaf")
    forward = [(i, i + 1) for i in range(count - 1)]
    backward = [(target, source) for source, target in forward]
    return forward, backward


def leaf_sum_kernel(member_ref, leaf_ref, low_ref, own_ref, high_ref):
    leaves = leaf_ref.shape[0]
    slots = own_ref.shape[0] + 2
    outs = [low_ref.at[0]] + [own_ref.at[t] for t in range(slots - 2)] + [high_ref.at[0]]
    for row in range(0, leaf_ref.shape[1], 8):
        terms = [leaf_ref[s, row : row + 8, :] for s in range(leaves)]
        for t in range(slots):
            total = terms[0] * member_ref[0, t]
            for s in range(1, leaves):
                total = total + terms[s] * member_ref[s, t]
            outs[t][row : row + 8, :] = total


def leaf_sums(member, leaf_value, par_dev):
    leaves, rows, states = leaf_value.shape
    tile = min(32, rows)
    block = lambda count: pl.BlockSpec((count, tile, states), lambda i: (0, i, 0))
    shape = lambda count: jax.ShapeDtypeStruct((count, rows, states), jnp.float32)
    return pl.pallas_call(
        leaf_sum_kernel,
        grid=(rows // tile,),
        in_specs=[pl.BlockSpec(memory_space=pltpu.SMEM), block(leaves)],
        out_specs=[block(1), block(par_dev), block(1)],
        out_shape=[shape(1), shape(par_dev), shape(1)],
        compiler_params=pltpu.CompilerParams(vmem_limit_bytes=32 * 2**20),
    )(member, leaf_value)


def inverse_kernel(cost_ref, map_ref, side_ref, inv_ref, hess):
    parents, _, inputs = side_ref.shape
    row = lax.broadcasted_iota(jnp.int32, (inputs, inputs), 0)
    col = lax.broadcasted_iota(jnp.int32, (inputs, inputs), 1)
    eye = (row == col).astype(jnp.float32)
    dot = lambda a, b: jnp.dot(a, b, precision=highest, preferred_element_type=jnp.float32)
    for p in range(parents):
        product = lax.dot_general(
            map_ref[...],
            side_ref[p],
            (((0,), (0,)), ((), ())),
            precision=highest,
            preferred_element_type=jnp.float32,
        )
        value = cost_ref[...] + product
        hess[p] = value
        bound = jnp.max(jnp.sum(jnp.abs(value), axis=0))
        inv_ref[p] = eye / bound

    def more(carry):
        turn, worst = carry
        return jnp.logical_and(turn < 64, worst > 1e-8)

    def step(carry):
        turn, _ = carry
        residual = [eye - dot(hess[p], inv_ref[p]) for p in range(parents)]
        for p in range(parents):
            inv_ref[p] = inv_ref[p] + dot(inv_ref[p], residual[p])
        worst = jnp.sum(residual[0] * residual[0])
        for p in range(1, parents):
            worst = jnp.maximum(worst, jnp.sum(residual[p] * residual[p]))
        return turn + 1, worst

    lax.while_loop(more, step, (jnp.int32(0), jnp.float32(jnp.inf)))


def inverses(input_cost, input_map, side):
    parents, _, inputs = side.shape
    return pl.pallas_call(
        inverse_kernel,
        in_specs=[pl.BlockSpec(memory_space=pltpu.VMEM)] * 3,
        out_specs=pl.BlockSpec(memory_space=pltpu.VMEM),
        out_shape=jax.ShapeDtypeStruct((parents, inputs, inputs), jnp.float32),
        scratch_shapes=[pltpu.VMEM((parents, inputs, inputs), jnp.float32)],
        compiler_params=pltpu.CompilerParams(vmem_limit_bytes=32 * 2**20),
        cost_estimate=pl.CostEstimate(
            flops=600 * parents * inputs**3, bytes_accessed=4 * 2**20, transcendentals=0
        ),
    )(input_cost, input_map, side)


def local(
    leaf_value,
    section_cost,
    input_cost,
    dynamics,
    input_map,
    parent_of,
    prob_weight,
    parent_state,
    disturbance,
):
    leaf_dev = leaf_value.shape[0]
    par_dev = parent_state.shape[0]
    slab_rows = leaf_value.shape[1]
    leaf_index = lax.axis_index("leaf")
    column = lax.axis_index("mat")
    count = lax.axis_size("mat")
    forward, backward = edge_rows(parent_state)
    row_start = column * slab_rows
    full_dyn = gathered_once(dynamics)
    weights = prob_weight.astype(jnp.float32)
    my_parents = lax.dynamic_slice_in_dim(parent_of, leaf_index * leaf_dev, leaf_dev, 0)
    my_weights = lax.dynamic_slice_in_dim(weights, leaf_index * leaf_dev, leaf_dev, 0)
    first_label = leaf_index * par_dev
    slot_ids = jnp.arange(par_dev + 2, dtype=jnp.int32)
    chosen = (my_parents - first_label + 1)[:, None] == slot_ids[None, :]
    member = jnp.where(chosen, my_weights[:, None], 0.0)
    labels = first_label + jnp.arange(par_dev, dtype=jnp.int32)
    totals = jnp.sum(
        jnp.where(parent_of[:, None] == labels[None, :], weights[:, None], 0.0), axis=0
    )
    low, own, top = leaf_sums(member, leaf_value, par_dev)
    from_low = lax.ppermute(top, "leaf", forward)
    from_high = lax.ppermute(low, "leaf", backward)
    pads = [jnp.zeros_like(own[:1])] * (par_dev - 1)
    beside = jnp.concatenate([from_low] + pads) + jnp.concatenate(pads + [from_high])
    expected = (own + beside) / totals[:, None, None]

    side_rows = jnp.einsum("prk,ka->pra", expected, input_map, precision=high)
    side = gathered(side_rows, "mat", 1)
    state = gathered(parent_state, "mat", 1)

    def value_block(target):
        columns = lax.dynamic_slice_in_dim(full_dyn, target * slab_rows, slab_rows, 1)
        return jnp.einsum("prk,kj->prj", expected, columns, precision=high)

    dyn_cols = lax.dynamic_slice_in_dim(full_dyn, row_start, slab_rows, 1)
    parts = []
    for step in shifts_of(count):
        block = value_block(lax.rem(column + step, count))
        parts.append((step, shifted(block, "mat", step)))
    shape = (par_dev, slab_rows * count, slab_rows)
    value_cols = lax.dynamic_update_slice_in_dim(
        jnp.zeros(shape, jnp.float32), value_block(column), row_start, 1
    )

    inv = inverses(input_cost, input_map, side)
    free_next = jnp.einsum("ij,pj->pi", full_dyn, state, precision=highest)
    pull = jnp.einsum("pka,pk->pa", side, free_next, precision=highest)
    control = -jnp.einsum("pab,pb->pa", inv, pull, precision=highest)
    input_rows = lax.dynamic_slice_in_dim(input_map, row_start, slab_rows, 0)
    following = lax.dynamic_slice_in_dim(free_next, row_start, slab_rows, 1) + jnp.einsum(
        "ra,pa->pr", input_rows, control, precision=highest
    )
    below = lax.ppermute(following[par_dev - 1 :], "leaf", forward)
    above = lax.ppermute(following[:1], "leaf", backward)

    coupling_rows = jnp.einsum("kr,pka->pra", dyn_cols, side, precision=high)
    gain_rows = -jnp.einsum("pra,pab->prb", coupling_rows, inv, precision=high)
    feedback = jnp.einsum("prb,pkb->prk", gain_rows, side, precision=high)

    for step, part in parts[:-1]:
        source = lax.rem(column + count - step, count)
        value_cols = lax.dynamic_update_slice_in_dim(value_cols, part, source * slab_rows, 1)
    closed = jnp.swapaxes(value_cols, 1, 2) + feedback
    new_value = section_cost[None] + jnp.einsum("prk,kj->prj", closed, full_dyn, precision=high)
    for step, part in parts[-1:]:
        source = lax.rem(column + count - step, count)
        rows = lax.dynamic_slice_in_dim(full_dyn, source * slab_rows, slab_rows, 0)
        new_value = new_value + jnp.einsum("pkr,kj->prj", part, rows, precision=high)

    extended = jnp.concatenate([below, following, above], axis=0)
    child_state = disturbance
    for t in range(par_dev + 2):
        child_state = child_state + jnp.where(chosen[:, t : t + 1], extended[t][None, :], 0.0)
    return (new_value, gain_rows, child_state)


def solution(mesh):
    in_specs = (
        P("leaf", "mat", None),
        P("mat", None),
        P(),
        P("mat", None),
        P(),
        P(),
        P(),
        P("leaf", "mat"),
        P("leaf", "mat"),
    )
    out_specs = (P("leaf", "mat", None), P("leaf", "mat", None), P("leaf", "mat"))
    return jax.shard_map(local, mesh=mesh, in_specs=in_specs, out_specs=out_specs, check_vma=False)
```

```python
import jax
import jax.numpy as jnp
from jax import lax
from jax.experimental import pallas as pl
from jax.experimental.pallas import tpu as pltpu
from jax.sharding import PartitionSpec as P

highest = lax.Precision.HIGHEST
high = lax.Precision.HIGH


def shifted(block, axis, step):
    count = lax.axis_size(axis)
    return lax.ppermute(block, axis, [(i, (i + step) % count) for i in range(count)])


def shifts_of(count):
    order = []
    for step in range(1, count // 2 + 1):
        order.append(step)
        if count - step != step:
            order.append(count - step)
    return order


def gathered(block, axis, dim):
    count, me, size = lax.axis_size(axis), lax.axis_index(axis), block.shape[dim]
    shape = block.shape[:dim] + (size * count,) + block.shape[dim + 1 :]
    whole = lax.dynamic_update_slice_in_dim(jnp.zeros(shape, block.dtype), block, me * size, dim)
    parts = [(step, shifted(block, axis, step)) for step in shifts_of(count)]
    for step, part in parts:
        source = lax.rem(me + count - step, count)
        whole = lax.dynamic_update_slice_in_dim(whole, part, source * size, dim)
    return whole


def quarter_start(block):
    leaves, quarter = lax.axis_size("leaf"), block.shape[0] // 4
    leaf = lax.axis_index("leaf")
    return (2 * (leaf // (leaves // 2)) + lax.rem(leaf, 2)) * quarter


def splits(block):
    return lax.axis_size("leaf") % 4 == 0 and block.shape[0] % 32 == 0


def quarters(block):
    mine = lax.dynamic_slice_in_dim(block, quarter_start(block), block.shape[0] // 4, 0)
    return [shifted(mine, "mat", step) for step in shifts_of(lax.axis_size("mat"))]


def swapped(block, own):
    leaves, count = lax.axis_size("leaf"), lax.axis_size("mat")
    size = block.shape[0]
    half, quarter = leaves // 2, size // 4
    leaf, me = lax.axis_index("leaf"), lax.axis_index("mat")
    upper, core = leaf // half, lax.rem(leaf, 2)
    across = [(i, (i + half) % leaves) for i in range(leaves)]
    beside = [(i, i ^ 1) for i in range(leaves)]
    shape = (size * count,) + block.shape[1:]
    whole = lax.dynamic_update_slice_in_dim(jnp.zeros(shape, block.dtype), block, me * size, 0)
    for step, part in zip(shifts_of(count), own):
        start = lax.rem(me + count - step, count) * size
        other = lax.ppermute(part, "leaf", across)
        pieces = (
            (part, upper, core),
            (other, 1 - upper, core),
            (lax.ppermute(part, "leaf", beside), upper, 1 - core),
            (lax.ppermute(other, "leaf", beside), 1 - upper, 1 - core),
        )
        for piece, high_half, side in pieces:
            at = start + (2 * high_half + side) * quarter
            whole = lax.dynamic_update_slice_in_dim(whole, piece, at, 0)
    return whole


def edge_rows(block):
    count = lax.axis_size("leaf")
    forward = [(i, i + 1) for i in range(count - 1)]
    backward = [(target, source) for source, target in forward]
    return forward, backward


def leaf_sum_kernel(member_ref, leaf_ref, low_ref, own_ref, high_ref):
    leaves = leaf_ref.shape[0]
    slots = own_ref.shape[0] + 2
    outs = [low_ref.at[0]] + [own_ref.at[t] for t in range(slots - 2)] + [high_ref.at[0]]
    for row in range(0, leaf_ref.shape[1], 8):
        terms = [leaf_ref[s, row : row + 8, :] for s in range(leaves)]
        for t in range(slots):
            total = terms[0] * member_ref[0, t]
            for s in range(1, leaves):
                total = total + terms[s] * member_ref[s, t]
            outs[t][row : row + 8, :] = total


def leaf_sums(member, leaf_value, par_dev):
    leaves, rows, states = leaf_value.shape
    tile = min(32, rows)
    block = lambda count: pl.BlockSpec((count, tile, states), lambda i: (0, i, 0))
    shape = lambda count: jax.ShapeDtypeStruct((count, rows, states), jnp.float32)
    return pl.pallas_call(
        leaf_sum_kernel,
        grid=(rows // tile,),
        in_specs=[pl.BlockSpec(memory_space=pltpu.SMEM), block(leaves)],
        out_specs=[block(1), block(par_dev), block(1)],
        out_shape=[shape(1), shape(par_dev), shape(1)],
        compiler_params=pltpu.CompilerParams(vmem_limit_bytes=32 * 2**20),
    )(member, leaf_value)


def inverse_kernel(cost_ref, map_ref, side_ref, inv_ref, hess):
    parents, _, inputs = side_ref.shape
    row = lax.broadcasted_iota(jnp.int32, (inputs, inputs), 0)
    col = lax.broadcasted_iota(jnp.int32, (inputs, inputs), 1)
    eye = (row == col).astype(jnp.float32)
    dot = lambda a, b: jnp.dot(a, b, precision=highest, preferred_element_type=jnp.float32)
    for p in range(parents):
        product = lax.dot_general(
            map_ref[...],
            side_ref[p],
            (((0,), (0,)), ((), ())),
            precision=highest,
            preferred_element_type=jnp.float32,
        )
        value = cost_ref[...] + product
        hess[p] = value
        bound = jnp.max(jnp.sum(jnp.abs(value), axis=0))
        inv_ref[p] = eye / bound

    def more(carry):
        turn, worst = carry
        return jnp.logical_and(turn < 64, worst > 1e-8)

    def step(carry):
        turn, _ = carry
        residual = [eye - dot(hess[p], inv_ref[p]) for p in range(parents)]
        for p in range(parents):
            inv_ref[p] = inv_ref[p] + dot(inv_ref[p], residual[p])
        worst = jnp.sum(residual[0] * residual[0])
        for p in range(1, parents):
            worst = jnp.maximum(worst, jnp.sum(residual[p] * residual[p]))
        return turn + 1, worst

    lax.while_loop(more, step, (jnp.int32(0), jnp.float32(jnp.inf)))


def inverses(input_cost, input_map, side):
    parents, _, inputs = side.shape
    return pl.pallas_call(
        inverse_kernel,
        in_specs=[pl.BlockSpec(memory_space=pltpu.VMEM)] * 3,
        out_specs=pl.BlockSpec(memory_space=pltpu.VMEM),
        out_shape=jax.ShapeDtypeStruct((parents, inputs, inputs), jnp.float32),
        scratch_shapes=[pltpu.VMEM((parents, inputs, inputs), jnp.float32)],
        compiler_params=pltpu.CompilerParams(vmem_limit_bytes=32 * 2**20),
        cost_estimate=pl.CostEstimate(
            flops=600 * parents * inputs**3, bytes_accessed=4 * 2**20, transcendentals=0
        ),
    )(input_cost, input_map, side)


def local(
    leaf_value,
    section_cost,
    input_cost,
    dynamics,
    input_map,
    parent_of,
    prob_weight,
    parent_state,
    disturbance,
):
    leaf_dev = leaf_value.shape[0]
    par_dev = parent_state.shape[0]
    slab_rows = leaf_value.shape[1]
    leaf_index = lax.axis_index("leaf")
    column = lax.axis_index("mat")
    count = lax.axis_size("mat")
    forward, backward = edge_rows(parent_state)
    row_start = column * slab_rows
    split = splits(dynamics)
    if split:
        own_quarters = quarters(dynamics)
    weights = prob_weight.astype(jnp.float32)
    my_parents = lax.dynamic_slice_in_dim(parent_of, leaf_index * leaf_dev, leaf_dev, 0)
    my_weights = lax.dynamic_slice_in_dim(weights, leaf_index * leaf_dev, leaf_dev, 0)
    first_label = leaf_index * par_dev
    slot_ids = jnp.arange(par_dev + 2, dtype=jnp.int32)
    chosen = (my_parents - first_label + 1)[:, None] == slot_ids[None, :]
    member = jnp.where(chosen, my_weights[:, None], 0.0)
    labels = first_label + jnp.arange(par_dev, dtype=jnp.int32)
    totals = jnp.sum(
        jnp.where(parent_of[:, None] == labels[None, :], weights[:, None], 0.0), axis=0
    )
    low, own, top = leaf_sums(member, leaf_value, par_dev)
    from_low = lax.ppermute(top, "leaf", forward)
    from_high = lax.ppermute(low, "leaf", backward)
    from_low, from_high, parent_state = lax.optimization_barrier(
        (from_low, from_high, parent_state)
    )
    if split:
        from_low, from_high, own_quarters = lax.optimization_barrier(
            (from_low, from_high, own_quarters)
        )
        full_dyn = swapped(dynamics, own_quarters)
    else:
        full_dyn = gathered(dynamics, "mat", 0)
    pads = [jnp.zeros_like(own[:1])] * (par_dev - 1)
    beside = jnp.concatenate([from_low] + pads) + jnp.concatenate(pads + [from_high])
    expected = (own + beside) / totals[:, None, None]

    side_rows = jnp.einsum("prk,ka->pra", expected, input_map, precision=high)
    side = gathered(side_rows, "mat", 1)
    state = gathered(parent_state, "mat", 1)

    def value_block(target):
        columns = lax.dynamic_slice_in_dim(full_dyn, target * slab_rows, slab_rows, 1)
        return jnp.einsum("prk,kj->prj", expected, columns, precision=high)

    dyn_cols = lax.dynamic_slice_in_dim(full_dyn, row_start, slab_rows, 1)
    parts = []
    for step in shifts_of(count):
        block = value_block(lax.rem(column + step, count))
        parts.append((step, shifted(block, "mat", step)))
    shape = (par_dev, slab_rows * count, slab_rows)
    value_cols = lax.dynamic_update_slice_in_dim(
        jnp.zeros(shape, jnp.float32), value_block(column), row_start, 1
    )

    inv = inverses(input_cost, input_map, side)
    free_next = jnp.einsum("ij,pj->pi", full_dyn, state, precision=highest)
    pull = jnp.einsum("pka,pk->pa", side, free_next, precision=highest)
    control = -jnp.einsum("pab,pb->pa", inv, pull, precision=highest)
    input_rows = lax.dynamic_slice_in_dim(input_map, row_start, slab_rows, 0)
    following = lax.dynamic_slice_in_dim(free_next, row_start, slab_rows, 1) + jnp.einsum(
        "ra,pa->pr", input_rows, control, precision=highest
    )
    below = lax.ppermute(following[par_dev - 1 :], "leaf", forward)
    above = lax.ppermute(following[:1], "leaf", backward)

    coupling_rows = jnp.einsum("kr,pka->pra", dyn_cols, side, precision=high)
    gain_rows = -jnp.einsum("pra,pab->prb", coupling_rows, inv, precision=high)
    feedback = jnp.einsum("prb,pkb->prk", gain_rows, side, precision=high)

    for step, part in parts[:-1]:
        source = lax.rem(column + count - step, count)
        value_cols = lax.dynamic_update_slice_in_dim(value_cols, part, source * slab_rows, 1)
    closed = jnp.swapaxes(value_cols, 1, 2) + feedback
    new_value = section_cost[None] + jnp.einsum("prk,kj->prj", closed, full_dyn, precision=high)
    for step, part in parts[-1:]:
        source = lax.rem(column + count - step, count)
        rows = lax.dynamic_slice_in_dim(full_dyn, source * slab_rows, slab_rows, 0)
        new_value = new_value + jnp.einsum("pkr,kj->prj", part, rows, precision=high)

    extended = jnp.concatenate([below, following, above], axis=0)
    child_state = disturbance
    for t in range(par_dev + 2):
        child_state = child_state + jnp.where(chosen[:, t : t + 1], extended[t][None, :], 0.0)
    return (new_value, gain_rows, child_state)


def solution(mesh):
    in_specs = (
        P("leaf", "mat", None),
        P("mat", None),
        P(),
        P("mat", None),
        P(),
        P(),
        P(),
        P("leaf", "mat"),
        P("leaf", "mat"),
    )
    out_specs = (P("leaf", "mat", None), P("leaf", "mat", None), P("leaf", "mat"))
    return jax.shard_map(local, mesh=mesh, in_specs=in_specs, out_specs=out_specs, check_vma=False)
```
